32 devices in a mesh: grp: 4 (over y, x), blk: 2 (over core), head: 4 (over z).
Axes of the slice: x: 2, y: 2, z: 4, core: 2. Of those that a mesh axis runs over, the one named last changes fastest.
Arguments:
- queries: bfloat16 [4096, 1024], P(('grp', 'blk', 'head')), may hold values from -6 to 6
- keys: bfloat16 [4096, 1024], P(('grp', 'blk', 'head')), may hold values from -6 to 6
- values: bfloat16 [4096, 1024], P(('grp', 'blk', 'head')), may hold values from -6 to 6
- out_grad: bfloat16 [4096, 1024], P(('grp', 'blk', 'head')), may hold values from -6 to 6
- segment: int32 [4096], P(('grp', 'blk', 'head')), may hold values from 0 to 3, never falling along the last dimension, each value on 1 to 2048 neighbouring positions
Outputs:
- attention_out: bfloat16 [4096, 1024], P(('grp', 'blk', 'head'))
- query_grad: bfloat16 [4096, 1024], P(('grp', 'blk', 'head'))
- key_grad: bfloat16 [4096, 1024], P(('grp', 'blk', 'head'))
- value_grad: bfloat16 [4096, 1024], P(('grp', 'blk', 'head'))
The draws below stay inside these ranges and needn't reach their ends.
Inputs may be any that keep to these rules, and one draw needn't show every extreme that they name: `segment`: never falls along the pack; every stream covers 1 to 2048 consecutive positions and one covers exactly 2048.
All inputs are finite; a program needn't handle non-finite values.
Results may differ from the reference program's by a relative error of at most 0.0049.
Values may be sent and summed in bfloat16 or wider, within the bound.
No kernel may reach another device: no remote copies, remote signals or barrier semaphores. Data moves between devices by JAX's collectives and lax.ppermute only.
A program may use at most 64 MiB of HBM per device.

```python
import math
import jax
import jax.numpy as jnp
import numpy as np
from jax import lax

TOK_DEV = 128
HEADS = 8
DH = 128
REACH = 4
MAXLEN = 2048
SEQ = 4096
STREAMS = 4
FEAT = 1024
N_HEAD = 4


def levels(key, shape, split, low, largest):
    def one(dim, shards_of):
        steps = jax.random.uniform(jax.random.fold_in(jax.random.fold_in(key, 6), dim), (shards_of,), jnp.float32, low / len(split), largest / len(split))
        return jnp.repeat(jnp.exp(steps), shape[dim] // shards_of).reshape((-1,) + (1,) * (len(shape) - dim - 1))

    gain = one(*split[0])
    for cut in split[1:]:
        gain = gain * one(*cut)
    return gain


def length_profile(number_of, total, bound, lean):
    weights = [(1 << 20) // math.isqrt(rank ** lean) + 1 for rank in range(2, number_of + 1)]
    surplus, given = total - bound - (number_of - 1), [1] * (number_of - 1)
    while surplus > 0:
        free = [i for i in range(number_of - 1) if given[i] < bound]
        whole, budget = sum([weights[i] for i in free]), surplus
        for i in free:
            addition = min(bound - given[i], max(1, budget * weights[i] // whole), surplus)
            given[i] = given[i] + addition
            surplus = surplus - addition
    return np.array([bound] + given)


def ragged(stream_key, count, total, most, skew):
    if count == 2:
        one = jax.random.randint(stream_key, (), max(1, total - most), min(most, total - 1) + 1)
        return jnp.stack([one, total - one])
    tallies = jnp.asarray(length_profile(count, total, most, skew), jnp.int32)
    couples = (count - 1) // 2
    giver, sink = tallies[1:1 + 2 * couples:2], tallies[2:2 + 2 * couples:2]
    room = jnp.minimum(giver - 1, most - sink)
    passed = jax.random.randint(jax.random.fold_in(stream_key, 1), (couples,), 0, 1 << 20) % (room + 1)
    tallies = tallies.at[1:1 + 2 * couples:2].set(giver - passed).at[2:2 + 2 * couples:2].set(sink + passed)
    return tallies[jax.random.permutation(jax.random.fold_in(stream_key, 2), count)]


def scatter_about(stream_key, extent, scale, most, split=(), kind=jnp.bfloat16):
    values = jax.random.normal(stream_key, extent, jnp.float32) * scale
    if len(split) > 0:
        values = levels(stream_key, extent, split, -0.22, 0.18) * values
    return jnp.clip(values, min=-most, max=most).astype(kind)


def setup_inputs(seed: int = 0) -> dict:
    seeds = jax.random.split(jax.random.key(seed), 6)
    queries = scatter_about(seeds[0], (SEQ, FEAT), 1.0, 6.0, ((0, 32),))
    keys = scatter_about(seeds[1], (SEQ, FEAT), 1.0, 6.0, ((0, 32),))
    values = scatter_about(seeds[2], (SEQ, FEAT), 1.0, 6.0, ((0, 32),))
    out_grad = scatter_about(seeds[3], (SEQ, FEAT), 1.0, 6.0, ((0, 32),))
    segment = jnp.searchsorted(jnp.cumsum(ragged(seeds[4], STREAMS, SEQ, MAXLEN, 2)), jnp.arange(SEQ), side="right").astype(jnp.int32)
    return dict(queries=queries, keys=keys, values=values, out_grad=out_grad, segment=segment)


def silu_parts(scores):
    logistic = jax.nn.sigmoid(scores)
    return (scores * logistic, logistic * (1.0 + scores * (1.0 - logistic)))

def reference(queries, keys, values, out_grad, segment):
    block_rows = N_HEAD * TOK_DEV
    block_count = SEQ // block_rows
    margin = REACH * block_rows
    window = margin + block_rows
    width = HEADS * DH
    score_scale = 1.0 / math.sqrt(DH)
    norm_factor = 1.0 / math.sqrt(MAXLEN)
    keys_padded = jnp.concatenate([jnp.zeros((margin, width), keys.dtype), keys], axis=0)
    values_padded = jnp.concatenate([jnp.zeros((margin, width), values.dtype), values], axis=0)
    seg_padded = jnp.concatenate([jnp.full((margin,), -1, jnp.int32), segment.astype(jnp.int32)], axis=0)
    causal = jnp.arange(window, dtype=jnp.int32)[None, :] <= jnp.arange(block_rows, dtype=jnp.int32)[:, None] + margin

    def split_heads(matrix):
        return matrix.reshape(matrix.shape[0], HEADS, DH).astype(jnp.float32)

    def one_block(carry, index):
        key_acc, value_acc = carry
        start = (index * block_rows).astype(jnp.int32)
        query = split_heads(lax.dynamic_slice_in_dim(queries, start, block_rows, 0))
        cotangent = split_heads(lax.dynamic_slice_in_dim(out_grad, start, block_rows, 0))
        seg_query = lax.dynamic_slice_in_dim(segment.astype(jnp.int32), start, block_rows, 0)
        key_block = split_heads(lax.dynamic_slice_in_dim(keys_padded, start, window, 0))
        value_block = split_heads(lax.dynamic_slice_in_dim(values_padded, start, window, 0))
        seg_key = lax.dynamic_slice_in_dim(seg_padded, start, window, 0)
        allowed = (seg_query[:, None] == seg_key[None, :]) & causal
        scores = jnp.einsum('qhd,khd->hqk', query, key_block) * score_scale
        active, slope = silu_parts(scores)
        weight = jnp.where(allowed[None], active * norm_factor, 0.0).astype(jnp.bfloat16)
        weight = lax.optimization_barrier(weight).astype(jnp.float32)
        dprob = jnp.einsum('qhd,khd->hqk', cotangent, value_block)
        dscore = jnp.where(allowed[None], dprob * slope * (norm_factor * score_scale), 0.0).astype(jnp.bfloat16)
        dscore = lax.optimization_barrier(dscore).astype(jnp.float32)
        output = jnp.einsum('hqk,khd->qhd', weight, value_block).reshape(block_rows, width)
        query_term = jnp.einsum('hqk,khd->qhd', dscore, key_block).reshape(block_rows, width)
        key_term = jnp.einsum('hqk,qhd->khd', dscore, query).reshape(window, width)
        value_term = jnp.einsum('hqk,qhd->khd', weight, cotangent).reshape(window, width)
        key_acc = lax.dynamic_update_slice_in_dim(key_acc, lax.dynamic_slice_in_dim(key_acc, start, window, 0) + key_term, start, 0)
        value_acc = lax.dynamic_update_slice_in_dim(value_acc, lax.dynamic_slice_in_dim(value_acc, start, window, 0) + value_term, start, 0)
        return ((key_acc, value_acc), (output.astype(jnp.bfloat16), query_term.astype(jnp.bfloat16)))
    start_acc = jnp.zeros((margin + SEQ, width), jnp.float32)
    (key_acc, value_acc), (outputs, query_terms) = lax.scan(one_block, (start_acc, start_acc), jnp.arange(block_count, dtype=jnp.int32))
    attention_out = outputs.reshape(SEQ, width)
    query_grad = query_terms.reshape(SEQ, width)
    key_grad = key_acc[margin:].astype(jnp.bfloat16)
    value_grad = value_acc[margin:].astype(jnp.bfloat16)
    return (attention_out, query_grad, key_grad, value_grad)
```

```python
import functools
import math

import jax
import jax.numpy as jnp
from jax import lax
from jax.experimental import pallas as pl
from jax.experimental.pallas import tpu as pltpu
from jax.sharding import Mesh, PartitionSpec as P

DH = 128
REACH = 4
PAIR = 2
CORE = 2
ROWS = 512
COLS = 512
STRIP = 32
PART = 128
MASKED = -1e6
CLEAR, MIXED = 0, 1
DEVICE_AXES = ("sup", "pair", "core", "head")
HEAD_AXES = ("head", "pair")
SEG_ROWS = 16
TAG_FLOPS = 40_000_000_000
ATTEND_VMEM = 24 * 1024 * 1024
MOVE_VMEM = 8 * 1024 * 1024
PACK_VMEM = 63 * 1024 * 1024


def run_copies(copies):
    for copy in copies:
        copy.start()
    for copy in copies:
        copy.wait()


def pack_kernel(queries, keys, values, out_grad, segment, packed, *scratch):
    held, numbers, places, sems = scratch[:4], *scratch[4:]
    heads = packed.shape[0]
    tokens = queries.shape[0]

    def copies_in(order):
        return [
            pltpu.make_async_copy(source, held[slot], sems.at[0, slot])
            for slot, source in enumerate(order)
        ]

    def start(order):
        for copy in copies_in(order):
            copy.start()

    first_keys = lax.axis_index("sup") % 2 == 0
    by_keys, by_queries = (keys, values, queries, out_grad), (queries, out_grad, keys, values)
    numbers_in = pltpu.make_async_copy(segment, numbers, sems.at[0, 4])
    numbers_in.start()

    @pl.when(first_keys)
    def _():
        start(by_keys)

    @pl.when(jnp.logical_not(first_keys))
    def _():
        start(by_queries)

    def copy_out(part, at, rows):
        rows = pl.ds(at, rows)
        return pltpu.make_async_copy(places.at[:, rows], packed.at[:, rows], sems.at[1, part])

    numbers_in.wait()
    places[:, pl.ds(2 * tokens, SEG_ROWS)] = jnp.broadcast_to(
        (numbers[...] + 1).astype(jnp.float32).astype(places.dtype)[None], (heads, SEG_ROWS, tokens)
    )
    outs = []
    for slot, copy_in in enumerate(copies_in(by_keys)):
        copy_in.wait()
        at = slot * tokens + (SEG_ROWS if slot > 1 else 0)
        for head in range(heads):
            places[head, pl.ds(at, tokens)] = held[slot][:, pl.ds(head * DH, DH)]
        outs.append(copy_out(slot, at, tokens + (SEG_ROWS if slot == 1 else 0)))
        outs[-1].start()
    for copy in outs:
        copy.wait()


def pack(queries, keys, values, out_grad, segment):
    tokens, features = queries.shape
    shape = (features // DH, 4 * tokens + SEG_ROWS, DH)
    anywhere = pl.BlockSpec(memory_space=pl.ANY)
    return pl.pallas_call(
        pack_kernel,
        out_shape=jax.ShapeDtypeStruct(shape, queries.dtype),
        in_specs=[anywhere] * 5,
        out_specs=anywhere,
        scratch_shapes=[pltpu.VMEM(queries.shape, queries.dtype)] * 4
        + [
            pltpu.VMEM(segment.shape, segment.dtype),
            pltpu.VMEM(shape, queries.dtype),
            pltpu.SemaphoreType.DMA((2, 5)),
        ],
        compiler_params=pltpu.CompilerParams(vmem_limit_bytes=PACK_VMEM),
    )(queries, keys, values, out_grad, segment)


def unpack_kernel(queries_on, back, *refs):
    outs, rows_out, sems = refs[-6:-2], refs[-2], refs[-1]
    heads = back.shape[0]
    tokens = rows_out.shape[1]
    of_queries = lax.axis_index("sup") % 2 == queries_on

    def copy_out(slot, target):
        return pltpu.make_async_copy(rows_out.at[slot], target, sems.at[slot])

    for slot, (by_query, by_key) in enumerate(((outs[0], outs[3]), (outs[1], outs[2]))):
        for head in range(heads):
            rows_out[slot, :, pl.ds(head * DH, DH)] = back[head, pl.ds(slot * tokens, tokens)]
        pl.when(of_queries)(lambda: copy_out(slot, by_query).start())
        pl.when(jnp.logical_not(of_queries))(lambda: copy_out(slot, by_key).start())
    for slot in range(2):
        copy_out(slot, outs[slot]).wait()


def unpack(queries_on, back, outs=()):
    heads, rows, _ = back.shape
    tokens = rows // 2
    anywhere = pl.BlockSpec(memory_space=pl.ANY)
    return pl.pallas_call(
        functools.partial(unpack_kernel, queries_on),
        out_shape=[jax.ShapeDtypeStruct((tokens, heads * DH), back.dtype)] * 4,
        in_specs=[pl.BlockSpec(memory_space=pltpu.VMEM)] + [anywhere] * len(outs),
        out_specs=[anywhere] * 4,
        scratch_shapes=[
            pltpu.VMEM((2, tokens, heads * DH), back.dtype),
            pltpu.SemaphoreType.DMA((2,)),
        ],
        input_output_aliases={1 + i: i for i in range(len(outs))},
        compiler_params=pltpu.CompilerParams(vmem_limit_bytes=MOVE_VMEM),
    )(back, *outs)


def tag_kernel(given, other, tag):
    tag[...] = given[...]


def later_tag(tag, other):
    vmem = pl.BlockSpec(memory_space=pltpu.VMEM)
    return pl.pallas_call(
        tag_kernel,
        out_shape=jax.ShapeDtypeStruct(tag.shape, tag.dtype),
        in_specs=[vmem, pl.BlockSpec(memory_space=pl.ANY)],
        out_specs=vmem,
        compiler_params=pltpu.CompilerParams(vmem_limit_bytes=MOVE_VMEM),
        cost_estimate=pl.CostEstimate(
            flops=TAG_FLOPS, bytes_accessed=2 * tag.size, transcendentals=0
        ),
    )(tag, other)


def attend_kernel(factors, slabs, forward, own_seg, other_seg, rows_slab, *refs):
    score_scale, norm = factors
    col_slabs = refs[: 2 * slabs]
    packed, *tag = refs[2 * slabs : -11]
    seg, seg_rows, seg_cols, row_one, row_two, col_one, col_two = refs[-11:-4]
    sum_one, sum_two, work, sem = refs[-4:]
    parity, core = lax.axis_index("sup") % 2, lax.axis_index("core")
    sign = (1 - 2 * parity) * (1 if forward else -1)
    chunks = rows_slab.shape[0]
    tokens = packed.shape[1] // 2
    half_rows = chunks // PAIR * tokens
    half_blocks = half_rows // COLS
    local_blocks = REACH * half_blocks
    row_blocks = chunks * tokens // ROWS
    col_chunks = COLS // tokens
    if tag:
        tag[0][...] = jnp.zeros_like(tag[0])

    def place_of(index, chunk):
        slab, owner = index // 2, (core if index % 2 == 0 else 1 - core)
        inner, pair = chunk // PAIR, chunk % PAIR
        return (slab * REACH + pair * CORE + owner) * (chunks // PAIR) + inner

    def row_of(chunk):
        return (chunk % PAIR * (chunks // PAIR) + chunk // PAIR) * tokens

    for index, source in enumerate(col_slabs):
        source, at = (source, 2 * tokens) if index > 1 else ((own_seg, other_seg)[index], 0)
        for chunk in range(chunks):
            numbers = source[chunk, pl.ds(at, SEG_ROWS)].astype(jnp.float32)[:1]
            place = place_of(index, chunk)
            lanes = pl.ds(chunk // PAIR % col_chunks * tokens, tokens)
            seg_cols[place // col_chunks, :, lanes] = numbers.astype(jnp.int32)
    to_scalars = pltpu.make_async_copy(seg_cols, seg, sem)
    to_scalars.start()
    for index, source in enumerate(col_slabs):
        for chunk in range(chunks):
            place = place_of(index, chunk)
            rows = pl.ds(chunk // PAIR % col_chunks * tokens, tokens)
            for slot, ref in enumerate((col_one, col_two)):
                ref[place // col_chunks, rows] = source[chunk, pl.ds(slot * tokens, tokens)]
    for chunk in range(chunks):
        for slot, ref in enumerate((row_one, row_two)):
            ref[pl.ds(row_of(chunk), tokens)] = rows_slab[chunk, pl.ds(slot * tokens, tokens)]

    def row_token_of(row_block):
        row_start = row_block * ROWS
        return (row_start // half_rows * CORE + core) * half_rows + row_start % half_rows

    def col_token_of(block):
        beyond = jnp.where(block >= local_blocks, 1, 0)
        return block * COLS - beyond * (sign + 1) * local_blocks * COLS

    def seg_at(token):
        return seg[token // COLS, 0, token % COLS]

    sum_one[...] = jnp.zeros_like(sum_one)
    sum_two[...] = jnp.zeros_like(sum_two)
    to_scalars.wait()
    total = 0
    for row_block in range(row_blocks):
        row_token = row_token_of(row_block)
        row_first, row_last = seg_at(row_token), seg_at(row_token + ROWS - 1)
        at_rows = row_block * ROWS

        @pl.when(row_first == row_last)
        def _():
            seg_rows[pl.ds(at_rows, ROWS)] = jnp.full((ROWS, DH), row_first, jnp.int32)

        @pl.when(row_first != row_last)
        def _():
            for chunk in range(chunks):
                if row_of(chunk) // ROWS != row_block:
                    continue
                numbers = own_seg[chunk].astype(jnp.float32)[:1]
                seg_rows[pl.ds(row_of(chunk), tokens)] = jnp.transpose(
                    jnp.broadcast_to(numbers, (DH, tokens))
                ).astype(jnp.int32)

        for block in range(slabs * local_blocks):
            col_token = col_token_of(block)
            col_first, col_last = seg[block, 0, 0], seg[block, 0, COLS - 1]
            touching = (col_last >= row_first) & (col_first <= row_last)
            ahead, behind = col_token - row_token, row_token + ROWS - col_token
            reached = jnp.where(sign > 0, behind > 0, ahead + COLS > 0)
            inside = jnp.where(sign > 0, ahead + COLS <= 1, behind <= 1)
            same = (row_first == row_last) & (col_first == row_first) & (col_last == row_first)
            work[0, total] = row_block
            work[1, total] = block
            work[2, total] = jnp.where(same & inside, CLEAR, MIXED)
            total = total + jnp.where(touching & reached, 1, 0)
    dims = (((1,), (1,)), ((), ()))

    def weigh(raw, dprob):
        logistic = pltpu.reciprocal(
            1.0 + jnp.exp2(raw * (-score_scale * math.log2(math.e))), approx=True
        )
        active = raw * logistic
        slope = logistic + active * score_scale * (1.0 - logistic)
        return (active * (score_scale * norm)).astype(jnp.bfloat16), (dprob * slope).astype(
            jnp.bfloat16
        )

    def tile(item, masked):
        row_block, block = work[0, item], work[1, item]
        if masked:
            offset = (col_token_of(block) - row_token_of(row_block)) * sign
            distance = (
                lax.broadcasted_iota(jnp.int32, (STRIP, DH), 0)
                - lax.broadcasted_iota(jnp.int32, (STRIP, DH), 1)
            ) * sign

        def products(part):
            at = pl.ds(pl.multiple_of(row_block * ROWS + part, PART), PART)
            return [
                lax.dot_general(rows[at], cols[block], dims, preferred_element_type=jnp.float32)
                for rows, cols in ((row_one, col_one), (row_two, col_two))
            ]

        ahead = products(0)
        for part in range(0, ROWS, PART):
            scores, dprobs = ahead
            if part + PART < ROWS:
                ahead = products(part + PART)
            weights, dscores = [], []
            for row in range(0, PART, STRIP):
                pieces = []
                if masked:
                    row_seg = seg_rows[pl.ds(row_block * ROWS + part + row, STRIP)]
                for col in range(0, COLS, DH):
                    raw = scores[row : row + STRIP, col : col + DH]
                    if masked:
                        col_seg = jnp.broadcast_to(seg_cols[block, :, pl.ds(col, DH)], (STRIP, DH))
                        allowed = (row_seg == col_seg) & (
                            distance >= offset - (part + row - col) * sign
                        )
                        raw = jnp.where(allowed, raw, MASKED)
                    pieces.append(weigh(raw, dprobs[row : row + STRIP, col : col + DH]))
                weights.append(jnp.concatenate([piece[0] for piece in pieces], axis=1))
                dscores.append(jnp.concatenate([piece[1] for piece in pieces], axis=1))
            for target, left, cols in ((sum_one, weights, col_two), (sum_two, dscores, col_one)):
                target[row_block, pl.ds(part, PART)] += jnp.dot(
                    jnp.concatenate(left, axis=0), cols[block], preferred_element_type=jnp.float32
                )

    def step(item, carry):
        clear = work[2, item] == CLEAR
        pl.when(clear)(functools.partial(tile, item, False))
        pl.when(jnp.logical_not(clear))(functools.partial(tile, item, True))
        return carry

    lax.fori_loop(0, total, step, 0)
    for chunk in range(chunks):
        row_block, inner = row_of(chunk) // ROWS, row_of(chunk) % ROWS
        at = pl.ds(inner, tokens)
        packed[chunk, pl.ds(0, tokens)] = sum_one[row_block, at].astype(packed.dtype)
        packed[chunk, pl.ds(tokens, tokens)] = (
            sum_two[row_block, at] * (norm * score_scale)
        ).astype(packed.dtype)


def attend(forward, rows_slab, col_slabs, local_segs):
    chunks = rows_slab.shape[0]
    rows = chunks * DH
    slabs = len(col_slabs) // 2
    reach = CORE * rows
    factors = (1.0 / math.sqrt(DH), 1.0 / math.sqrt(reach))
    vmem = pl.BlockSpec(memory_space=pltpu.VMEM)
    dtype = rows_slab.dtype
    blocks = slabs * reach // COLS
    row_blocks = rows // ROWS
    sums = jax.ShapeDtypeStruct((chunks, 2 * rows // chunks, DH), dtype)
    tag = [jax.ShapeDtypeStruct((1, 1, DH), jnp.float32)] if forward else []
    return pl.pallas_call(
        functools.partial(attend_kernel, factors, slabs, forward),
        out_shape=[sums] + tag,
        in_specs=[vmem] * (3 + 2 * slabs),
        out_specs=[vmem] * (1 + len(tag)),
        scratch_shapes=[
            pltpu.SMEM((blocks, 1, COLS), jnp.int32),
            pltpu.VMEM((rows, DH), jnp.int32),
            pltpu.VMEM((blocks, 1, COLS), jnp.int32),
            pltpu.VMEM((rows, DH), dtype),
            pltpu.VMEM((rows, DH), dtype),
            pltpu.VMEM((blocks, COLS, DH), dtype),
            pltpu.VMEM((blocks, COLS, DH), dtype),
        ]
        + [
            pltpu.VMEM((row_blocks, ROWS, DH), jnp.float32),
            pltpu.VMEM((row_blocks, ROWS, DH), jnp.float32),
            pltpu.SMEM((3, row_blocks * blocks + 1), jnp.int32),
            pltpu.SemaphoreType.DMA(()),
        ],
        compiler_params=pltpu.CompilerParams(vmem_limit_bytes=ATTEND_VMEM),
        cost_estimate=pl.CostEstimate(
            flops=8 * DH * rows * reach * slabs if forward else 0,
            bytes_accessed=8 * rows_slab.size if forward else 0,
            transcendentals=rows * reach * slabs if forward else 0,
        ),
    )(*local_segs, rows_slab, *col_slabs)


def shards(queries, keys, values, out_grad, segment):
    sups = lax.axis_size("sup")
    tokens = queries.shape[0]

    def over_heads(packed):
        return lax.all_to_all(packed, HEAD_AXES, split_axis=0, concat_axis=0, tiled=True)

    def with_other_core(slab):
        return [slab, lax.ppermute(slab, "core", [(0, 1), (1, 0)])]

    def over_sups(slab, start):
        pairs = [(i, i + 1) for i in range(start, sups - 1, 2)]
        return lax.ppermute(slab, "sup", pairs + [(b, a) for a, b in pairs])

    slab = over_heads(pack(queries, keys, values, out_grad, segment[None]))
    first_own, second_own = slab[:, : 2 * tokens + SEG_ROWS], slab[:, 2 * tokens + SEG_ROWS :]
    first_cols = with_other_core(first_own)
    beyond = over_sups(first_own, 0)
    second_cols = with_other_core(second_own)
    local_segs = [slab[:, 2 * tokens :] for slab in first_cols]
    first_all = first_cols
    if sups > 2:
        later = over_sups(jnp.concatenate([second_own, local_segs[0]], axis=1), 1)
        first_all = first_cols + with_other_core(later)
    first_sums, tag = attend(True, second_own, first_all, local_segs)
    first_back = over_heads(first_sums)
    beyond_cols = with_other_core(beyond + later_tag(tag, second_cols[1]).astype(beyond.dtype))
    (second_sums,) = attend(False, first_own, second_cols + beyond_cols, local_segs)
    second_back = over_heads(second_sums)
    return tuple(unpack(1, second_back, unpack(0, first_back)))


def solution(mesh):
    blocks = mesh.shape["grp"] * mesh.shape["blk"]
    grid = Mesh(
        mesh.devices.reshape(blocks // REACH, PAIR, CORE, mesh.shape["head"]), DEVICE_AXES
    )
    rows = P(DEVICE_AXES, None)
    return jax.shard_map(
        shards,
        mesh=grid,
        in_specs=(rows, rows, rows, rows, P(DEVICE_AXES)),
        out_specs=(rows, rows, rows, rows),
        check_vma=False,
    )
```

```python
import functools
import math

import jax
import jax.numpy as jnp
from jax import lax
from jax.experimental import pallas as pl
from jax.experimental.pallas import tpu as pltpu
from jax.sharding import Mesh, PartitionSpec as P

DH = 128
REACH = 4
PAIR = 2
CORE = 2
ROWS = 512
COLS = 512
STRIP = 32
PART = 256
MASKED = -1e6
CLEAR, MIXED = 0, 1
DEVICE_AXES = ("sup", "pair", "core", "head")
HEAD_AXES = ("head", "pair")
SEG_ROWS = 16
TAG_FLOPS = 40_000_000_000
ATTEND_VMEM = 24 * 1024 * 1024
MOVE_VMEM = 8 * 1024 * 1024
PACK_VMEM = 63 * 1024 * 1024


def run_copies(copies):
    for copy in copies:
        copy.start()
    for copy in copies:
        copy.wait()


def pack_kernel(queries, keys, values, out_grad, segment, packed, *scratch):
    held, numbers, places, sems = scratch[:4], *scratch[4:]
    heads = packed.shape[0]
    tokens = queries.shape[0]

    def copies_in(order):
        return [
            pltpu.make_async_copy(source, held[slot], sems.at[0, slot])
            for slot, source in enumerate(order)
        ]

    def start(order):
        for copy in copies_in(order):
            copy.start()

    first_keys = lax.axis_index("sup") % 2 == 0
    by_keys, by_queries = (keys, values, queries, out_grad), (queries, out_grad, keys, values)
    numbers_in = pltpu.make_async_copy(segment, numbers, sems.at[0, 4])
    numbers_in.start()

    @pl.when(first_keys)
    def _():
        start(by_keys)

    @pl.when(jnp.logical_not(first_keys))
    def _():
        start(by_queries)

    def copy_out(part, at, rows):
        rows = pl.ds(at, rows)
        return pltpu.make_async_copy(places.at[:, rows], packed.at[:, rows], sems.at[1, part])

    numbers_in.wait()
    places[:, pl.ds(2 * tokens, SEG_ROWS)] = jnp.broadcast_to(
        (numbers[...] + 1).astype(jnp.float32).astype(places.dtype)[None], (heads, SEG_ROWS, tokens)
    )
    outs = []
    for slot, copy_in in enumerate(copies_in(by_keys)):
        copy_in.wait()
        at = slot * tokens + (SEG_ROWS if slot > 1 else 0)
        for head in range(heads):
            places[head, pl.ds(at, tokens)] = held[slot][:, pl.ds(head * DH, DH)]
        outs.append(copy_out(slot, at, tokens + (SEG_ROWS if slot == 1 else 0)))
        outs[-1].start()
    for copy in outs:
        copy.wait()


def pack(queries, keys, values, out_grad, segment):
    tokens, features = queries.shape
    shape = (features // DH, 4 * tokens + SEG_ROWS, DH)
    anywhere = pl.BlockSpec(memory_space=pl.ANY)
    return pl.pallas_call(
        pack_kernel,
        out_shape=jax.ShapeDtypeStruct(shape, queries.dtype),
        in_specs=[anywhere] * 5,
        out_specs=anywhere,
        scratch_shapes=[pltpu.VMEM(queries.shape, queries.dtype)] * 4
        + [
            pltpu.VMEM(segment.shape, segment.dtype),
            pltpu.VMEM(shape, queries.dtype),
            pltpu.SemaphoreType.DMA((2, 5)),
        ],
        compiler_params=pltpu.CompilerParams(vmem_limit_bytes=PACK_VMEM),
    )(queries, keys, values, out_grad, segment)


def unpack_kernel(queries_on, back, *refs):
    outs, rows_out, sems = refs[-6:-2], refs[-2], refs[-1]
    heads = back.shape[0]
    tokens = rows_out.shape[1]
    of_queries = lax.axis_index("sup") % 2 == queries_on

    def copy_out(slot, target):
        return pltpu.make_async_copy(rows_out.at[slot], target, sems.at[slot])

    for slot, (by_query, by_key) in enumerate(((outs[0], outs[3]), (outs[1], outs[2]))):
        for head in range(heads):
            rows_out[slot, :, pl.ds(head * DH, DH)] = back[head, pl.ds(slot * tokens, tokens)]
        pl.when(of_queries)(lambda: copy_out(slot, by_query).start())
        pl.when(jnp.logical_not(of_queries))(lambda: copy_out(slot, by_key).start())
    for slot in range(2):
        copy_out(slot, outs[slot]).wait()


def unpack(queries_on, back, outs=()):
    heads, rows, _ = back.shape
    tokens = rows // 2
    anywhere = pl.BlockSpec(memory_space=pl.ANY)
    return pl.pallas_call(
        functools.partial(unpack_kernel, queries_on),
        out_shape=[jax.ShapeDtypeStruct((tokens, heads * DH), back.dtype)] * 4,
        in_specs=[pl.BlockSpec(memory_space=pltpu.VMEM)] + [anywhere] * len(outs),
        out_specs=[anywhere] * 4,
        scratch_shapes=[
            pltpu.VMEM((2, tokens, heads * DH), back.dtype),
            pltpu.SemaphoreType.DMA((2,)),
        ],
        input_output_aliases={1 + i: i for i in range(len(outs))},
        compiler_params=pltpu.CompilerParams(vmem_limit_bytes=MOVE_VMEM),
    )(back, *outs)


def tag_kernel(given, other, tag):
    tag[...] = given[...]


def later_tag(tag, other):
    vmem = pl.BlockSpec(memory_space=pltpu.VMEM)
    return pl.pallas_call(
        tag_kernel,
        out_shape=jax.ShapeDtypeStruct(tag.shape, tag.dtype),
        in_specs=[vmem, pl.BlockSpec(memory_space=pl.ANY)],
        out_specs=vmem,
        compiler_params=pltpu.CompilerParams(vmem_limit_bytes=MOVE_VMEM),
        cost_estimate=pl.CostEstimate(
            flops=TAG_FLOPS, bytes_accessed=2 * tag.size, transcendentals=0
        ),
    )(tag, other)


def attend_kernel(factors, slabs, forward, own_seg, other_seg, rows_slab, *refs):
    score_scale, norm = factors
    col_slabs = refs[: 2 * slabs]
    packed, *tag = refs[2 * slabs : -11]
    seg, seg_rows, seg_cols, row_one, row_two, col_one, col_two = refs[-11:-4]
    sum_one, sum_two, work, sem = refs[-4:]
    parity, core = lax.axis_index("sup") % 2, lax.axis_index("core")
    sign = (1 - 2 * parity) * (1 if forward else -1)
    chunks = rows_slab.shape[0]
    tokens = packed.shape[1] // 2
    half_rows = chunks // PAIR * tokens
    half_blocks = half_rows // COLS
    local_blocks = REACH * half_blocks
    row_blocks = chunks * tokens // ROWS
    col_chunks = COLS // tokens
    if tag:
        tag[0][...] = jnp.zeros_like(tag[0])

    def place_of(index, chunk):
        slab, owner = index // 2, (core if index % 2 == 0 else 1 - core)
        inner, pair = divmod(chunks - 1 - chunk, PAIR)
        return (slab * REACH + pair * CORE + owner) * (chunks // PAIR) + inner

    def row_of(chunk):
        inner, pair = divmod(chunks - 1 - chunk, PAIR)
        return (pair * (chunks // PAIR) + inner) * tokens

    for index, source in enumerate(col_slabs):
        source, at = (source, 2 * tokens) if index > 1 else ((own_seg, other_seg)[index], 0)
        for chunk in range(chunks):
            numbers = source[chunk, pl.ds(at, SEG_ROWS)].astype(jnp.float32)[:1]
            place = place_of(index, chunk)
            lanes = pl.ds(row_of(chunk) % COLS, tokens)
            seg_cols[place // col_chunks, :, lanes] = numbers.astype(jnp.int32)
    to_scalars = pltpu.make_async_copy(seg_cols, seg, sem)
    to_scalars.start()
    for index, source in enumerate(col_slabs):
        for chunk in range(chunks):
            place = place_of(index, chunk)
            rows = pl.ds(row_of(chunk) % COLS, tokens)
            for slot, ref in enumerate((col_one, col_two)):
                ref[place // col_chunks, rows] = source[chunk, pl.ds(slot * tokens, tokens)]
    for chunk in range(chunks):
        for slot, ref in enumerate((row_one, row_two)):
            ref[pl.ds(row_of(chunk), tokens)] = rows_slab[chunk, pl.ds(slot * tokens, tokens)]

    def row_token_of(row_block):
        row_start = row_block * ROWS
        return (row_start // half_rows * CORE + core) * half_rows + row_start % half_rows

    def col_token_of(block):
        beyond = jnp.where(block >= local_blocks, 1, 0)
        return block * COLS - beyond * (sign + 1) * local_blocks * COLS

    def seg_at(token):
        return seg[token // COLS, 0, token % COLS]

    sum_one[...] = jnp.zeros_like(sum_one)
    sum_two[...] = jnp.zeros_like(sum_two)
    to_scalars.wait()
    total = 0
    for row_block in range(row_blocks):
        row_token = row_token_of(row_block)
        row_first, row_last = seg_at(row_token), seg_at(row_token + ROWS - 1)
        at_rows = row_block * ROWS

        @pl.when(row_first == row_last)
        def _():
            seg_rows[pl.ds(at_rows, ROWS)] = jnp.full((ROWS, DH), row_first, jnp.int32)

        @pl.when(row_first != row_last)
        def _():
            for chunk in range(chunks):
                if row_of(chunk) // ROWS != row_block:
                    continue
                numbers = own_seg[chunk].astype(jnp.float32)[:1]
                seg_rows[pl.ds(row_of(chunk), tokens)] = jnp.transpose(
                    jnp.broadcast_to(numbers, (DH, tokens))
                ).astype(jnp.int32)

        for block in range(slabs * local_blocks):
            col_token = col_token_of(block)
            col_first, col_last = seg[block, 0, 0], seg[block, 0, COLS - 1]
            touching = (col_last >= row_first) & (col_first <= row_last)
            ahead, behind = col_token - row_token, row_token + ROWS - col_token
            reached = jnp.where(sign > 0, behind > 0, ahead + COLS > 0)
            inside = jnp.where(sign > 0, ahead + COLS <= 1, behind <= 1)
            same = (row_first == row_last) & (col_first == row_first) & (col_last == row_first)
            work[0, total] = row_block
            work[1, total] = block
            work[2, total] = jnp.where(same & inside, CLEAR, MIXED)
            total = total + jnp.where(touching & reached, 1, 0)
    dims = (((1,), (1,)), ((), ()))

    def weigh(raw, dprob):
        logistic = pltpu.reciprocal(
            1.0 + jnp.exp2(raw * (-score_scale * math.log2(math.e))), approx=True
        )
        active = raw * logistic
        slope = logistic + active * score_scale * (1.0 - logistic)
        return (active * (score_scale * norm)).astype(jnp.bfloat16), (dprob * slope).astype(
            jnp.bfloat16
        )

    def tile(item, masked):
        row_block, block = work[0, item], work[1, item]
        if masked:
            offset = (col_token_of(block) - row_token_of(row_block)) * sign
            distance = (
                lax.broadcasted_iota(jnp.int32, (STRIP, DH), 0)
                - lax.broadcasted_iota(jnp.int32, (STRIP, DH), 1)
            ) * sign
        for part in range(0, ROWS, PART):
            at = pl.ds(pl.multiple_of(row_block * ROWS + part, PART), PART)
            scores, dprobs = [
                lax.dot_general(rows[at], cols[block], dims, preferred_element_type=jnp.float32)
                for rows, cols in ((row_one, col_one), (row_two, col_two))
            ]
            weights, dscores = [], []
            for row in range(0, PART, STRIP):
                pieces = []
                if masked:
                    row_seg = seg_rows[pl.ds(row_block * ROWS + part + row, STRIP)]
                for col in range(0, COLS, DH):
                    raw = scores[row : row + STRIP, col : col + DH]
                    if masked:
                        col_seg = jnp.broadcast_to(seg_cols[block, :, pl.ds(col, DH)], (STRIP, DH))
                        allowed = (row_seg == col_seg) & (
                            distance >= offset - (part + row - col) * sign
                        )
                        raw = jnp.where(allowed, raw, MASKED)
                    pieces.append(weigh(raw, dprobs[row : row + STRIP, col : col + DH]))
                weights.append(jnp.concatenate([piece[0] for piece in pieces], axis=1))
                dscores.append(jnp.concatenate([piece[1] for piece in pieces], axis=1))
            for target, left, cols in ((sum_one, weights, col_two), (sum_two, dscores, col_one)):
                target[row_block, pl.ds(part, PART)] += jnp.dot(
                    jnp.concatenate(left, axis=0), cols[block], preferred_element_type=jnp.float32
                )

    def step(item, carry):
        clear = work[2, item] == CLEAR
        pl.when(clear)(functools.partial(tile, item, False))
        pl.when(jnp.logical_not(clear))(functools.partial(tile, item, True))
        return carry

    lax.fori_loop(0, total, step, 0)
    for chunk in range(chunks):
        row_block, inner = row_of(chunk) // ROWS, row_of(chunk) % ROWS
        at = pl.ds(inner, tokens)
        packed[chunk, pl.ds(0, tokens)] = sum_one[row_block, at].astype(packed.dtype)
        packed[chunk, pl.ds(tokens, tokens)] = (
            sum_two[row_block, at] * (norm * score_scale)
        ).astype(packed.dtype)


def attend(forward, rows_slab, col_slabs, local_segs):
    chunks = rows_slab.shape[0]
    rows = chunks * DH
    slabs = len(col_slabs) // 2
    reach = CORE * rows
    factors = (1.0 / math.sqrt(DH), 1.0 / math.sqrt(reach))
    vmem = pl.BlockSpec(memory_space=pltpu.VMEM)
    dtype = rows_slab.dtype
    blocks = slabs * reach // COLS
    row_blocks = rows // ROWS
    sums = jax.ShapeDtypeStruct((chunks, 2 * rows // chunks, DH), dtype)
    tag = [jax.ShapeDtypeStruct((1, 1, DH), jnp.float32)] if forward else []
    return pl.pallas_call(
        functools.partial(attend_kernel, factors, slabs, forward),
        out_shape=[sums] + tag,
        in_specs=[vmem] * (3 + 2 * slabs),
        out_specs=[vmem] * (1 + len(tag)),
        scratch_shapes=[
            pltpu.SMEM((blocks, 1, COLS), jnp.int32),
            pltpu.VMEM((rows, DH), jnp.int32),
            pltpu.VMEM((blocks, 1, COLS), jnp.int32),
            pltpu.VMEM((rows, DH), dtype),
            pltpu.VMEM((rows, DH), dtype),
            pltpu.VMEM((blocks, COLS, DH), dtype),
            pltpu.VMEM((blocks, COLS, DH), dtype),
        ]
        + [
            pltpu.VMEM((row_blocks, ROWS, DH), jnp.float32),
            pltpu.VMEM((row_blocks, ROWS, DH), jnp.float32),
            pltpu.SMEM((3, row_blocks * blocks + 1), jnp.int32),
            pltpu.SemaphoreType.DMA(()),
        ],
        compiler_params=pltpu.CompilerParams(vmem_limit_bytes=ATTEND_VMEM),
        cost_estimate=pl.CostEstimate(
            flops=8 * DH * rows * reach * slabs if forward else 0,
            bytes_accessed=8 * rows_slab.size if forward else 0,
            transcendentals=rows * reach * slabs if forward else 0,
        ),
    )(*local_segs, rows_slab, *col_slabs)


def shards(queries, keys, values, out_grad, segment):
    sups = lax.axis_size("sup")
    tokens = queries.shape[0]

    def over_heads(packed):
        return lax.all_to_all(
            packed,
            HEAD_AXES,
            split_axis=0,
            concat_axis=0,
            axis_index_groups=[list(range(packed.shape[0]))[::-1]],
            tiled=True,
        )

    def with_other_core(slab):
        return [slab, lax.ppermute(slab, "core", [(0, 1), (1, 0)])]

    def over_sups(slab, start):
        pairs = [(i, i + 1) for i in range(start, sups - 1, 2)]
        return lax.ppermute(slab, "sup", pairs + [(b, a) for a, b in pairs])

    slab = over_heads(pack(queries, keys, values, out_grad, segment[None]))
    first_own, second_own = slab[:, : 2 * tokens + SEG_ROWS], slab[:, 2 * tokens + SEG_ROWS :]
    first_cols = with_other_core(first_own)
    beyond = over_sups(first_own, 0)
    second_cols = with_other_core(second_own)
    local_segs = [slab[:, 2 * tokens :] for slab in first_cols]
    first_all = first_cols
    if sups > 2:
        later = over_sups(jnp.concatenate([second_own, local_segs[0]], axis=1), 1)
        first_all = first_cols + with_other_core(later)
    first_sums, tag = attend(True, second_own, first_all, local_segs)
    first_back = over_heads(first_sums)
    beyond_cols = with_other_core(beyond + later_tag(tag, second_cols[1]).astype(beyond.dtype))
    (second_sums,) = attend(False, first_own, second_cols + beyond_cols, local_segs)
    second_back = over_heads(second_sums)
    return tuple(unpack(1, second_back, unpack(0, first_back)))


def solution(mesh):
    blocks = mesh.shape["grp"] * mesh.shape["blk"]
    grid = Mesh(
        mesh.devices.reshape(blocks // REACH, PAIR, CORE, mesh.shape["head"]), DEVICE_AXES
    )
    rows = P(DEVICE_AXES, None)
    return jax.shard_map(
        shards,
        mesh=grid,
        in_specs=(rows, rows, rows, rows, P(DEVICE_AXES)),
        out_specs=(rows, rows, rows, rows),
        check_vma=False,
    )
```

```python
import functools
import math

import jax
import jax.numpy as jnp
from jax import lax
from jax.experimental import pallas as pl
from jax.experimental.pallas import tpu as pltpu
from jax.sharding import Mesh, PartitionSpec as P

DH = 128
REACH = 4
PAIR = 2
CORE = 2
ROWS = 512
COLS = 512
STRIP = 32
PART = 256
MASKED = -1e6
CLEAR, MIXED, LOWER, UPPER = range(4)
DEVICE_AXES = ("sup", "pair", "core", "head")
HEAD_AXES = ("head", "pair")
SEG_ROWS = 16
TAG_FLOPS = 40_000_000_000
ATTEND_VMEM = 24 * 1024 * 1024
MOVE_VMEM = 8 * 1024 * 1024
PACK_VMEM = 63 * 1024 * 1024


def run_copies(copies):
    for copy in copies:
        copy.start()
    for copy in copies:
        copy.wait()


def listed(count):
    return [(index + count // 2) % count for index in range(count)]


def pack_kernel(queries, keys, values, out_grad, segment, packed, *scratch):
    held, numbers, places, sems = scratch[:4], *scratch[4:]
    heads = packed.shape[0]
    tokens = queries.shape[0]

    def copies_in(order):
        return [
            pltpu.make_async_copy(source, held[slot], sems.at[0, slot])
            for slot, source in enumerate(order)
        ]

    def start(order):
        for copy in copies_in(order):
            copy.start()

    first_keys = lax.axis_index("sup") % 2 == 0
    by_keys, by_queries = (keys, values, queries, out_grad), (queries, out_grad, keys, values)
    numbers_in = pltpu.make_async_copy(segment, numbers, sems.at[0, 4])
    numbers_in.start()

    @pl.when(first_keys)
    def _():
        start(by_keys)

    @pl.when(jnp.logical_not(first_keys))
    def _():
        start(by_queries)

    def copy_out(part, at, rows):
        rows = pl.ds(at, rows)
        return pltpu.make_async_copy(places.at[:, rows], packed.at[:, rows], sems.at[1, part])

    numbers_in.wait()
    places[:, pl.ds(2 * tokens, SEG_ROWS)] = jnp.broadcast_to(
        (numbers[...] + 1).astype(jnp.float32).astype(places.dtype)[None], (heads, SEG_ROWS, tokens)
    )
    outs = []
    for slot, copy_in in enumerate(copies_in(by_keys)):
        copy_in.wait()
        at = slot * tokens + (SEG_ROWS if slot > 1 else 0)
        for head in range(heads):
            places[head, pl.ds(at, tokens)] = held[slot][:, pl.ds(head * DH, DH)]
        outs.append(copy_out(slot, at, tokens + (SEG_ROWS if slot == 1 else 0)))
        outs[-1].start()
    for copy in outs:
        copy.wait()


def pack(queries, keys, values, out_grad, segment):
    tokens, features = queries.shape
    shape = (features // DH, 4 * tokens + SEG_ROWS, DH)
    anywhere = pl.BlockSpec(memory_space=pl.ANY)
    return pl.pallas_call(
        pack_kernel,
        out_shape=jax.ShapeDtypeStruct(shape, queries.dtype),
        in_specs=[anywhere] * 5,
        out_specs=anywhere,
        scratch_shapes=[pltpu.VMEM(queries.shape, queries.dtype)] * 4
        + [
            pltpu.VMEM(segment.shape, segment.dtype),
            pltpu.VMEM(shape, queries.dtype),
            pltpu.SemaphoreType.DMA((2, 5)),
        ],
        compiler_params=pltpu.CompilerParams(vmem_limit_bytes=PACK_VMEM),
    )(queries, keys, values, out_grad, segment)


def unpack_kernel(queries_on, back, *refs):
    outs, rows_out, sems = refs[-6:-2], refs[-2], refs[-1]
    heads = back.shape[0]
    tokens = rows_out.shape[1]
    of_queries = lax.axis_index("sup") % 2 == queries_on

    def copy_out(slot, target):
        return pltpu.make_async_copy(rows_out.at[slot], target, sems.at[slot])

    for slot, (by_query, by_key) in enumerate(((outs[0], outs[3]), (outs[1], outs[2]))):
        for head in range(heads):
            rows_out[slot, :, pl.ds(head * DH, DH)] = back[head, pl.ds(slot * tokens, tokens)]
        pl.when(of_queries)(lambda: copy_out(slot, by_query).start())
        pl.when(jnp.logical_not(of_queries))(lambda: copy_out(slot, by_key).start())
    for slot in range(2):
        copy_out(slot, outs[slot]).wait()


def unpack(queries_on, back, outs=()):
    heads, rows, _ = back.shape
    tokens = rows // 2
    anywhere = pl.BlockSpec(memory_space=pl.ANY)
    return pl.pallas_call(
        functools.partial(unpack_kernel, queries_on),
        out_shape=[jax.ShapeDtypeStruct((tokens, heads * DH), back.dtype)] * 4,
        in_specs=[pl.BlockSpec(memory_space=pltpu.VMEM)] + [anywhere] * len(outs),
        out_specs=[anywhere] * 4,
        scratch_shapes=[
            pltpu.VMEM((2, tokens, heads * DH), back.dtype),
            pltpu.SemaphoreType.DMA((2,)),
        ],
        input_output_aliases={1 + i: i for i in range(len(outs))},
        compiler_params=pltpu.CompilerParams(vmem_limit_bytes=MOVE_VMEM),
    )(back, *outs)


def tag_kernel(given, other, tag):
    tag[...] = given[...]


def later_tag(tag, other):
    vmem = pl.BlockSpec(memory_space=pltpu.VMEM)
    return pl.pallas_call(
        tag_kernel,
        out_shape=jax.ShapeDtypeStruct(tag.shape, tag.dtype),
        in_specs=[vmem, pl.BlockSpec(memory_space=pl.ANY)],
        out_specs=vmem,
        compiler_params=pltpu.CompilerParams(vmem_limit_bytes=MOVE_VMEM),
        cost_estimate=pl.CostEstimate(
            flops=TAG_FLOPS, bytes_accessed=2 * tag.size, transcendentals=0
        ),
    )(tag, other)


def attend_kernel(factors, slabs, forward, own_seg, other_seg, rows_slab, *refs):
    score_scale, norm = factors
    col_slabs = refs[: 2 * slabs]
    packed, *tag = refs[2 * slabs : -11]
    seg, seg_rows, seg_cols, row_one, row_two, col_one, col_two = refs[-11:-4]
    sum_one, sum_two, work, sem = refs[-4:]
    parity, core = lax.axis_index("sup") % 2, lax.axis_index("core")
    sign = (1 - 2 * parity) * (1 if forward else -1)
    chunks = rows_slab.shape[0]
    tokens = packed.shape[1] // 2
    half_rows = chunks // PAIR * tokens
    half_blocks = half_rows // COLS
    local_blocks = REACH * half_blocks
    row_blocks = chunks * tokens // ROWS
    col_chunks = COLS // tokens
    if tag:
        tag[0][...] = jnp.zeros_like(tag[0])

    def place_of(index, chunk):
        slab, owner = index // 2, (core if index % 2 == 0 else 1 - core)
        inner, pair = divmod(listed(chunks)[chunk], PAIR)
        return (slab * REACH + pair * CORE + owner) * (chunks // PAIR) + inner

    def row_of(chunk):
        inner, pair = divmod(listed(chunks)[chunk], PAIR)
        return (pair * (chunks // PAIR) + inner) * tokens

    for index, source in enumerate(col_slabs):
        source, at = (source, 2 * tokens) if index > 1 else ((own_seg, other_seg)[index], 0)
        for chunk in range(chunks):
            numbers = source[chunk, pl.ds(at, SEG_ROWS)].astype(jnp.float32)[:1]
            place = place_of(index, chunk)
            lanes = pl.ds(row_of(chunk) % COLS, tokens)
            seg_cols[place // col_chunks, :, lanes] = numbers.astype(jnp.int32)
    to_scalars = pltpu.make_async_copy(seg_cols, seg, sem)
    to_scalars.start()
    for index, source in enumerate(col_slabs):
        for chunk in range(chunks):
            place = place_of(index, chunk)
            rows = pl.ds(row_of(chunk) % COLS, tokens)
            for slot, ref in enumerate((col_one, col_two)):
                ref[place // col_chunks, rows] = source[chunk, pl.ds(slot * tokens, tokens)]
    for chunk in range(chunks):
        for slot, ref in enumerate((row_one, row_two)):
            ref[pl.ds(row_of(chunk), tokens)] = rows_slab[chunk, pl.ds(slot * tokens, tokens)]

    def row_token_of(row_block):
        row_start = row_block * ROWS
        return (row_start // half_rows * CORE + core) * half_rows + row_start % half_rows

    def col_token_of(block):
        beyond = jnp.where(block >= local_blocks, 1, 0)
        return block * COLS - beyond * (sign + 1) * local_blocks * COLS

    def seg_at(token):
        return seg[token // COLS, 0, token % COLS]

    sum_one[...] = jnp.zeros_like(sum_one)
    sum_two[...] = jnp.zeros_like(sum_two)
    to_scalars.wait()
    total = 0
    for row_block in range(row_blocks):
        row_token = row_token_of(row_block)
        row_first, row_last = seg_at(row_token), seg_at(row_token + ROWS - 1)
        at_rows = row_block * ROWS

        @pl.when(row_first == row_last)
        def _():
            seg_rows[pl.ds(at_rows, ROWS)] = jnp.full((ROWS, DH), row_first, jnp.int32)

        @pl.when(row_first != row_last)
        def _():
            for chunk in range(chunks):
                if row_of(chunk) // ROWS != row_block:
                    continue
                numbers = own_seg[chunk].astype(jnp.float32)[:1]
                seg_rows[pl.ds(row_of(chunk), tokens)] = jnp.transpose(
                    jnp.broadcast_to(numbers, (DH, tokens))
                ).astype(jnp.int32)

        for block in range(slabs * local_blocks):
            col_token = col_token_of(block)
            col_first, col_last = seg[block, 0, 0], seg[block, 0, COLS - 1]
            touching = (col_last >= row_first) & (col_first <= row_last)
            ahead, behind = col_token - row_token, row_token + ROWS - col_token
            reached = jnp.where(sign > 0, behind > 0, ahead + COLS > 0)
            same = (row_first == row_last) & (col_first == row_first) & (col_last == row_first)
            work[0, total] = row_block
            work[1, total] = block
            work[2, total] = jnp.where(
                ahead == 0, jnp.where(sign > 0, LOWER, UPPER), jnp.where(same, CLEAR, MIXED)
            )
            total = total + jnp.where(touching & reached, 1, 0)
    dims = (((1,), (1,)), ((), ()))

    def weigh(raw, dprob):
        logistic = pltpu.reciprocal(
            1.0 + jnp.exp2(raw * (-score_scale * math.log2(math.e))), approx=True
        )
        active = raw * logistic
        slope = logistic + active * score_scale * (1.0 - logistic)
        return (active * (score_scale * norm)).astype(jnp.bfloat16), (dprob * slope).astype(
            jnp.bfloat16
        )

    def tile(item, kind):
        row_block, block = work[0, item], work[1, item]
        distance = lax.broadcasted_iota(jnp.int32, (STRIP, DH), 0) - lax.broadcasted_iota(
            jnp.int32, (STRIP, DH), 1
        )
        for part in range(0, ROWS, PART):
            at = pl.ds(pl.multiple_of(row_block * ROWS + part, PART), PART)
            scores, dprobs = [
                lax.dot_general(rows[at], cols[block], dims, preferred_element_type=jnp.float32)
                for rows, cols in ((row_one, col_one), (row_two, col_two))
            ]
            weights, dscores = [], []
            for row in range(0, PART, STRIP):
                weight, dscore = [], []
                if kind != CLEAR:
                    row_seg = seg_rows[pl.ds(row_block * ROWS + part + row, STRIP)]
                for col in range(0, COLS, DH):
                    shift = col - part - row
                    if kind == LOWER and shift >= STRIP or kind == UPPER and shift <= -DH:
                        weight.append(jnp.zeros((STRIP, DH), jnp.bfloat16))
                        dscore.append(weight[-1])
                        continue
                    raw = scores[row : row + STRIP, col : col + DH]
                    if kind != CLEAR:
                        allowed = row_seg == jnp.broadcast_to(
                            seg_cols[block, :, pl.ds(col, DH)], (STRIP, DH)
                        )
                        if kind == LOWER and shift > -DH:
                            allowed = allowed & (distance >= shift)
                        if kind == UPPER and shift < STRIP:
                            allowed = allowed & (distance <= shift)
                        raw = jnp.where(allowed, raw, MASKED)
                    pieces = weigh(raw, dprobs[row : row + STRIP, col : col + DH])
                    weight.append(pieces[0])
                    dscore.append(pieces[1])
                weights.append(jnp.concatenate(weight, axis=1))
                dscores.append(jnp.concatenate(dscore, axis=1))
            for target, left, cols in ((sum_one, weights, col_two), (sum_two, dscores, col_one)):
                target[row_block, pl.ds(part, PART)] += jnp.dot(
                    jnp.concatenate(left, axis=0), cols[block], preferred_element_type=jnp.float32
                )

    def step(item, carry):
        for kind in (CLEAR, MIXED, LOWER, UPPER):
            pl.when(work[2, item] == kind)(functools.partial(tile, item, kind))
        return carry

    lax.fori_loop(0, total, step, 0)
    for chunk in range(chunks):
        row_block, inner = row_of(chunk) // ROWS, row_of(chunk) % ROWS
        at = pl.ds(inner, tokens)
        packed[chunk, pl.ds(0, tokens)] = sum_one[row_block, at].astype(packed.dtype)
        packed[chunk, pl.ds(tokens, tokens)] = (
            sum_two[row_block, at] * (norm * score_scale)
        ).astype(packed.dtype)


def attend(forward, rows_slab, col_slabs, local_segs):
    chunks = rows_slab.shape[0]
    rows = chunks * DH
    slabs = len(col_slabs) // 2
    reach = CORE * rows
    factors = (1.0 / math.sqrt(DH), 1.0 / math.sqrt(reach))
    vmem = pl.BlockSpec(memory_space=pltpu.VMEM)
    dtype = rows_slab.dtype
    blocks = slabs * reach // COLS
    row_blocks = rows // ROWS
    sums = jax.ShapeDtypeStruct((chunks, 2 * rows // chunks, DH), dtype)
    tag = [jax.ShapeDtypeStruct((1, 1, DH), jnp.float32)] if forward else []
    return pl.pallas_call(
        functools.partial(attend_kernel, factors, slabs, forward),
        out_shape=[sums] + tag,
        in_specs=[vmem] * (3 + 2 * slabs),
        out_specs=[vmem] * (1 + len(tag)),
        scratch_shapes=[
            pltpu.SMEM((blocks, 1, COLS), jnp.int32),
            pltpu.VMEM((rows, DH), jnp.int32),
            pltpu.VMEM((blocks, 1, COLS), jnp.int32),
            pltpu.VMEM((rows, DH), dtype),
            pltpu.VMEM((rows, DH), dtype),
            pltpu.VMEM((blocks, COLS, DH), dtype),
            pltpu.VMEM((blocks, COLS, DH), dtype),
        ]
        + [
            pltpu.VMEM((row_blocks, ROWS, DH), jnp.float32),
            pltpu.VMEM((row_blocks, ROWS, DH), jnp.float32),
            pltpu.SMEM((3, row_blocks * blocks + 1), jnp.int32),
            pltpu.SemaphoreType.DMA(()),
        ],
        compiler_params=pltpu.CompilerParams(vmem_limit_bytes=ATTEND_VMEM),
        cost_estimate=pl.CostEstimate(
            flops=8 * DH * rows * reach * slabs if forward else 0,
            bytes_accessed=8 * rows_slab.size if forward else 0,
            transcendentals=rows * reach * slabs if forward else 0,
        ),
    )(*local_segs, rows_slab, *col_slabs)


def shards(queries, keys, values, out_grad, segment):
    sups = lax.axis_size("sup")
    tokens = queries.shape[0]

    def over_heads(packed):
        return lax.all_to_all(
            packed,
            HEAD_AXES,
            split_axis=0,
            concat_axis=0,
            axis_index_groups=[listed(packed.shape[0])],
            tiled=True,
        )

    def with_other_core(slab):
        return [slab, lax.ppermute(slab, "core", [(0, 1), (1, 0)])]

    def over_sups(slab, start):
        pairs = [(i, i + 1) for i in range(start, sups - 1, 2)]
        return lax.ppermute(slab, "sup", pairs + [(b, a) for a, b in pairs])

    slab = over_heads(pack(queries, keys, values, out_grad, segment[None]))
    first_own, second_own = slab[:, : 2 * tokens + SEG_ROWS], slab[:, 2 * tokens + SEG_ROWS :]
    first_cols = with_other_core(first_own)
    beyond = over_sups(first_own, 0)
    second_cols = with_other_core(second_own)
    local_segs = [slab[:, 2 * tokens :] for slab in first_cols]
    first_all = first_cols
    if sups > 2:
        later = over_sups(jnp.concatenate([second_own, local_segs[0]], axis=1), 1)
        first_all = first_cols + with_other_core(later)
    first_sums, tag = attend(True, second_own, first_all, local_segs)
    first_back = over_heads(first_sums)
    beyond_cols = with_other_core(beyond + later_tag(tag, second_cols[1]).astype(beyond.dtype))
    (second_sums,) = attend(False, first_own, second_cols + beyond_cols, local_segs)
    second_back = over_heads(second_sums)
    return tuple(unpack(1, second_back, unpack(0, first_back)))


def solution(mesh):
    blocks = mesh.shape["grp"] * mesh.shape["blk"]
    grid = Mesh(
        mesh.devices.reshape(blocks // REACH, PAIR, CORE, mesh.shape["head"]), DEVICE_AXES
    )
    rows = P(DEVICE_AXES, None)
    return jax.shard_map(
        shards,
        mesh=grid,
        in_specs=(rows, rows, rows, rows, P(DEVICE_AXES)),
        out_specs=(rows, rows, rows, rows),
        check_vma=False,
    )
```

```python
import functools
import math

import jax
import jax.numpy as jnp
from jax import lax
from jax.experimental import pallas as pl
from jax.experimental.pallas import tpu as pltpu
from jax.sharding import Mesh, PartitionSpec as P

DH = 128
REACH = 4
PAIR = 2
CORE = 2
ROWS = 512
COLS = 512
STRIP = 32
PART = 256
MASKED = -1e6
CLEAR, MIXED = 0, 1
DEVICE_AXES = ("sup", "pair", "core", "head")
HEAD_AXES = ("head", "pair")
SEG_ROWS = 16
SECOND_FLOPS = 40_000_000_000
OUTPUTS = {"first": ("packed", "tag"), "second": ("sums", "sums", "tag"), "last": ("packed",)}
ATTEND_VMEM = 24 * 1024 * 1024
MOVE_VMEM = 8 * 1024 * 1024
PACK_VMEM = 63 * 1024 * 1024


def run_copies(copies):
    for copy in copies:
        copy.start()
    for copy in copies:
        copy.wait()


def listed(count):
    return [(index + count // 2) % count for index in range(count)]


def pack_kernel(queries, keys, values, out_grad, segment, packed, *scratch):
    held, numbers, places, sems = scratch[:4], *scratch[4:]
    heads = packed.shape[0]
    tokens = queries.shape[0]

    def copies_in(order):
        return [
            pltpu.make_async_copy(source, held[slot], sems.at[0, slot])
            for slot, source in enumerate(order)
        ]

    def start(order):
        for copy in copies_in(order):
            copy.start()

    first_keys = lax.axis_index("sup") % 2 == 0
    by_keys, by_queries = (keys, values, queries, out_grad), (queries, out_grad, keys, values)
    numbers_in = pltpu.make_async_copy(segment, numbers, sems.at[0, 4])
    numbers_in.start()

    @pl.when(first_keys)
    def _():
        start(by_keys)

    @pl.when(jnp.logical_not(first_keys))
    def _():
        start(by_queries)

    def copy_out(part, at, rows):
        rows = pl.ds(at, rows)
        return pltpu.make_async_copy(places.at[:, rows], packed.at[:, rows], sems.at[1, part])

    numbers_in.wait()
    places[:, pl.ds(2 * tokens, SEG_ROWS)] = jnp.broadcast_to(
        (numbers[...] + 1).astype(jnp.float32).astype(places.dtype)[None], (heads, SEG_ROWS, tokens)
    )
    outs = []
    for slot, copy_in in enumerate(copies_in(by_keys)):
        copy_in.wait()
        at = slot * tokens + (SEG_ROWS if slot > 1 else 0)
        for head in range(heads):
            places[head, pl.ds(at, tokens)] = held[slot][:, pl.ds(head * DH, DH)]
        outs.append(copy_out(slot, at, tokens + (SEG_ROWS if slot == 1 else 0)))
        outs[-1].start()
    for copy in outs:
        copy.wait()


def pack(queries, keys, values, out_grad, segment):
    tokens, features = queries.shape
    shape = (features // DH, 4 * tokens + SEG_ROWS, DH)
    anywhere = pl.BlockSpec(memory_space=pl.ANY)
    return pl.pallas_call(
        pack_kernel,
        out_shape=jax.ShapeDtypeStruct(shape, queries.dtype),
        in_specs=[anywhere] * 5,
        out_specs=anywhere,
        scratch_shapes=[pltpu.VMEM(queries.shape, queries.dtype)] * 4
        + [
            pltpu.VMEM(segment.shape, segment.dtype),
            pltpu.VMEM(shape, queries.dtype),
            pltpu.SemaphoreType.DMA((2, 5)),
        ],
        compiler_params=pltpu.CompilerParams(vmem_limit_bytes=PACK_VMEM),
    )(queries, keys, values, out_grad, segment)


def unpack_kernel(queries_on, back, *refs):
    outs, rows_out, sems = refs[-6:-2], refs[-2], refs[-1]
    heads = back.shape[0]
    tokens = rows_out.shape[1]
    of_queries = lax.axis_index("sup") % 2 == queries_on

    def copy_out(slot, target):
        return pltpu.make_async_copy(rows_out.at[slot], target, sems.at[slot])

    for slot, (by_query, by_key) in enumerate(((outs[0], outs[3]), (outs[1], outs[2]))):
        for head in range(heads):
            rows_out[slot, :, pl.ds(head * DH, DH)] = back[head, pl.ds(slot * tokens, tokens)]
        pl.when(of_queries)(lambda: copy_out(slot, by_query).start())
        pl.when(jnp.logical_not(of_queries))(lambda: copy_out(slot, by_key).start())
    for slot in range(2):
        copy_out(slot, outs[slot]).wait()


def unpack(queries_on, back, outs=()):
    heads, rows, _ = back.shape
    tokens = rows // 2
    anywhere = pl.BlockSpec(memory_space=pl.ANY)
    return pl.pallas_call(
        functools.partial(unpack_kernel, queries_on),
        out_shape=[jax.ShapeDtypeStruct((tokens, heads * DH), back.dtype)] * 4,
        in_specs=[pl.BlockSpec(memory_space=pltpu.VMEM)] + [anywhere] * len(outs),
        out_specs=[anywhere] * 4,
        scratch_shapes=[
            pltpu.VMEM((2, tokens, heads * DH), back.dtype),
            pltpu.SemaphoreType.DMA((2,)),
        ],
        input_output_aliases={1 + i: i for i in range(len(outs))},
        compiler_params=pltpu.CompilerParams(vmem_limit_bytes=MOVE_VMEM),
    )(back, *outs)


def attend_kernel(factors, slabs, step_name, own_seg, other_seg, rows_slab, *refs):
    score_scale, norm = factors
    forward, skipped = step_name == "first", 2 if step_name == "last" else 0
    col_slabs, refs = refs[: 2 * slabs - skipped], refs[2 * slabs - skipped :]
    given, outs = refs[: -11 - len(OUTPUTS[step_name])], refs[-11 - len(OUTPUTS[step_name]) : -11]
    seg, seg_rows, seg_cols, row_one, row_two, col_one, col_two = refs[-11:-4]
    sum_one, sum_two, work, sem = refs[-4:]
    parity, core = lax.axis_index("sup") % 2, lax.axis_index("core")
    sign = (1 - 2 * parity) * (1 if forward else -1)
    chunks = rows_slab.shape[0]
    tokens = own_seg.shape[2]
    half_rows = chunks // PAIR * tokens
    half_blocks = half_rows // COLS
    local_blocks = REACH * half_blocks
    row_blocks = chunks * tokens // ROWS
    col_chunks = COLS // tokens
    first_block = local_blocks if skipped else 0
    if step_name == "first":
        outs[1][...] = jnp.zeros_like(outs[1])
    if step_name == "second":
        outs[2][...] = given[0][...]

    def place_of(index, chunk):
        slab, owner = index // 2, (core if index % 2 == 0 else 1 - core)
        inner, pair = divmod(listed(chunks)[chunk], PAIR)
        return (slab * REACH + pair * CORE + owner) * (chunks // PAIR) + inner

    def row_of(chunk):
        inner, pair = divmod(listed(chunks)[chunk], PAIR)
        return (pair * (chunks // PAIR) + inner) * tokens

    for index in range(2 * slabs):
        local = index < 2
        source = (own_seg, other_seg)[index] if local else col_slabs[index - skipped]
        at = 0 if local else 2 * tokens
        for chunk in range(chunks):
            numbers = source[chunk, pl.ds(at, SEG_ROWS)].astype(jnp.float32)[:1]
            place = place_of(index, chunk)
            lanes = pl.ds(row_of(chunk) % COLS, tokens)
            seg_cols[place // col_chunks, :, lanes] = numbers.astype(jnp.int32)
    to_scalars = pltpu.make_async_copy(seg_cols, seg, sem)
    to_scalars.start()
    for index, source in enumerate(col_slabs, skipped):
        for chunk in range(chunks):
            place = place_of(index, chunk) - first_block * col_chunks
            rows = pl.ds(row_of(chunk) % COLS, tokens)
            for slot, ref in enumerate((col_one, col_two)):
                ref[place // col_chunks, rows] = source[chunk, pl.ds(slot * tokens, tokens)]
    for chunk in range(chunks):
        for slot, ref in enumerate((row_one, row_two)):
            ref[pl.ds(row_of(chunk), tokens)] = rows_slab[chunk, pl.ds(slot * tokens, tokens)]

    def row_token_of(row_block):
        row_start = row_block * ROWS
        return (row_start // half_rows * CORE + core) * half_rows + row_start % half_rows

    def col_token_of(block):
        beyond = jnp.where(block >= local_blocks, 1, 0)
        return block * COLS - beyond * (sign + 1) * local_blocks * COLS

    def seg_at(token):
        return seg[token // COLS, 0, token % COLS]

    for index, ref in enumerate((sum_one, sum_two)):
        ref[...] = given[index][...] if step_name == "last" else jnp.zeros_like(ref)
    to_scalars.wait()
    total = 0
    for row_block in range(row_blocks):
        row_token = row_token_of(row_block)
        row_first, row_last = seg_at(row_token), seg_at(row_token + ROWS - 1)
        at_rows = row_block * ROWS

        @pl.when(row_first == row_last)
        def _():
            seg_rows[pl.ds(at_rows, ROWS)] = jnp.full((ROWS, DH), row_first, jnp.int32)

        @pl.when(row_first != row_last)
        def _():
            for chunk in range(chunks):
                if row_of(chunk) // ROWS != row_block:
                    continue
                numbers = own_seg[chunk].astype(jnp.float32)[:1]
                seg_rows[pl.ds(row_of(chunk), tokens)] = jnp.transpose(
                    jnp.broadcast_to(numbers, (DH, tokens))
                ).astype(jnp.int32)

        for block in range(first_block, slabs * local_blocks):
            col_token = col_token_of(block)
            col_first, col_last = seg[block, 0, 0], seg[block, 0, COLS - 1]
            touching = (col_last >= row_first) & (col_first <= row_last)
            ahead, behind = col_token - row_token, row_token + ROWS - col_token
            reached = jnp.where(sign > 0, behind > 0, ahead + COLS > 0)
            inside = jnp.where(sign > 0, ahead + COLS <= 1, behind <= 1)
            same = (row_first == row_last) & (col_first == row_first) & (col_last == row_first)
            work[0, total] = row_block
            work[1, total] = block
            work[2, total] = jnp.where(same & inside, CLEAR, MIXED)
            total = total + jnp.where(touching & reached, 1, 0)
    dims = (((1,), (1,)), ((), ()))

    def weigh(raw, dprob):
        logistic = pltpu.reciprocal(
            1.0 + jnp.exp2(raw * (-score_scale * math.log2(math.e))), approx=True
        )
        active = raw * logistic
        slope = logistic + active * score_scale * (1.0 - logistic)
        return (active * (score_scale * norm)).astype(jnp.bfloat16), (dprob * slope).astype(
            jnp.bfloat16
        )

    def tile(item, masked):
        row_block, block = work[0, item], work[1, item]
        held = block - first_block
        if masked:
            offset = (col_token_of(block) - row_token_of(row_block)) * sign
            distance = (
                lax.broadcasted_iota(jnp.int32, (STRIP, DH), 0)
                - lax.broadcasted_iota(jnp.int32, (STRIP, DH), 1)
            ) * sign
        for part in range(0, ROWS, PART):
            at = pl.ds(pl.multiple_of(row_block * ROWS + part, PART), PART)
            scores, dprobs = [
                lax.dot_general(rows[at], cols[held], dims, preferred_element_type=jnp.float32)
                for rows, cols in ((row_one, col_one), (row_two, col_two))
            ]
            weights, dscores = [], []
            for row in range(0, PART, STRIP):
                pieces = []
                if masked:
                    row_seg = seg_rows[pl.ds(row_block * ROWS + part + row, STRIP)]
                for col in range(0, COLS, DH):
                    raw = scores[row : row + STRIP, col : col + DH]
                    if masked:
                        col_seg = jnp.broadcast_to(seg_cols[block, :, pl.ds(col, DH)], (STRIP, DH))
                        allowed = (row_seg == col_seg) & (
                            distance >= offset - (part + row - col) * sign
                        )
                        raw = jnp.where(allowed, raw, MASKED)
                    pieces.append(weigh(raw, dprobs[row : row + STRIP, col : col + DH]))
                weights.append(jnp.concatenate([piece[0] for piece in pieces], axis=1))
                dscores.append(jnp.concatenate([piece[1] for piece in pieces], axis=1))
            for target, left, cols in ((sum_one, weights, col_two), (sum_two, dscores, col_one)):
                target[row_block, pl.ds(part, PART)] += jnp.dot(
                    jnp.concatenate(left, axis=0), cols[held], preferred_element_type=jnp.float32
                )

    def step(item, carry):
        clear = work[2, item] == CLEAR
        pl.when(clear)(functools.partial(tile, item, False))
        pl.when(jnp.logical_not(clear))(functools.partial(tile, item, True))
        return carry

    lax.fori_loop(0, total, step, 0)
    if step_name == "second":
        outs[0][...] = sum_one[...]
        outs[1][...] = sum_two[...]
        return
    packed = outs[0]
    for chunk in range(chunks):
        row_block, inner = row_of(chunk) // ROWS, row_of(chunk) % ROWS
        at = pl.ds(inner, tokens)
        packed[chunk, pl.ds(0, tokens)] = sum_one[row_block, at].astype(packed.dtype)
        packed[chunk, pl.ds(tokens, tokens)] = (
            sum_two[row_block, at] * (norm * score_scale)
        ).astype(packed.dtype)


def attend(step_name, rows_slab, col_slabs, local_segs, given=()):
    chunks = rows_slab.shape[0]
    rows = chunks * DH
    skipped = 2 if step_name == "last" else 0
    slabs = (len(col_slabs) + skipped) // 2
    reach = CORE * rows
    factors = (1.0 / math.sqrt(DH), 1.0 / math.sqrt(reach))
    vmem = pl.BlockSpec(memory_space=pltpu.VMEM)
    dtype = rows_slab.dtype
    blocks = slabs * reach // COLS
    row_blocks = rows // ROWS
    outputs = {
        "packed": jax.ShapeDtypeStruct((chunks, 2 * rows // chunks, DH), dtype),
        "sums": jax.ShapeDtypeStruct((row_blocks, ROWS, DH), jnp.float32),
        "tag": jax.ShapeDtypeStruct((1, 1, DH), jnp.float32),
    }
    outputs = [outputs[name] for name in OUTPUTS[step_name]]
    flops = {"first": 8 * DH * rows * reach * slabs, "second": SECOND_FLOPS, "last": 0}[step_name]
    return pl.pallas_call(
        functools.partial(attend_kernel, factors, slabs, step_name),
        out_shape=outputs,
        in_specs=[vmem] * (3 + len(col_slabs) + len(given)),
        out_specs=[vmem] * len(outputs),
        scratch_shapes=[
            pltpu.SMEM((blocks, 1, COLS), jnp.int32),
            pltpu.VMEM((rows, DH), jnp.int32),
            pltpu.VMEM((blocks, 1, COLS), jnp.int32),
            pltpu.VMEM((rows, DH), dtype),
            pltpu.VMEM((rows, DH), dtype),
            pltpu.VMEM((len(col_slabs) * rows // COLS, COLS, DH), dtype),
            pltpu.VMEM((len(col_slabs) * rows // COLS, COLS, DH), dtype),
        ]
        + [
            pltpu.VMEM((row_blocks, ROWS, DH), jnp.float32),
            pltpu.VMEM((row_blocks, ROWS, DH), jnp.float32),
            pltpu.SMEM((3, row_blocks * blocks + 1), jnp.int32),
            pltpu.SemaphoreType.DMA(()),
        ],
        compiler_params=pltpu.CompilerParams(vmem_limit_bytes=ATTEND_VMEM),
        cost_estimate=pl.CostEstimate(flops=flops, bytes_accessed=0, transcendentals=0),
    )(*local_segs, rows_slab, *col_slabs, *given)


def shards(queries, keys, values, out_grad, segment):
    sups = lax.axis_size("sup")
    tokens = queries.shape[0]

    def over_heads(packed):
        return lax.all_to_all(
            packed,
            HEAD_AXES,
            split_axis=0,
            concat_axis=0,
            axis_index_groups=[listed(packed.shape[0])],
            tiled=True,
        )

    def with_other_core(slab):
        return [slab, lax.ppermute(slab, "core", [(0, 1), (1, 0)])]

    def over_sups(slab, start):
        pairs = [(i, i + 1) for i in range(start, sups - 1, 2)]
        return lax.ppermute(slab, "sup", pairs + [(b, a) for a, b in pairs])

    slab = over_heads(pack(queries, keys, values, out_grad, segment[None]))
    first_own, second_own = slab[:, : 2 * tokens + SEG_ROWS], slab[:, 2 * tokens + SEG_ROWS :]
    first_cols = with_other_core(first_own)
    beyond = over_sups(first_own, 0)
    second_cols = with_other_core(second_own)
    local_segs = [slab[:, 2 * tokens :] for slab in first_cols]
    first_all = first_cols
    if sups > 2:
        later = over_sups(jnp.concatenate([second_own, local_segs[0]], axis=1), 1)
        first_all = first_cols + with_other_core(later)
    first_sums, tag = attend("first", second_own, first_all, local_segs)
    first_back = over_heads(first_sums)
    *local_sums, tag = attend("second", first_own, second_cols, local_segs, (tag,))
    beyond_cols = with_other_core(beyond + tag.astype(beyond.dtype))
    (second_sums,) = attend("last", first_own, beyond_cols, local_segs, local_sums)
    second_back = over_heads(second_sums)
    return tuple(unpack(1, second_back, unpack(0, first_back)))


def solution(mesh):
    blocks = mesh.shape["grp"] * mesh.shape["blk"]
    grid = Mesh(
        mesh.devices.reshape(blocks // REACH, PAIR, CORE, mesh.shape["head"]), DEVICE_AXES
    )
    rows = P(DEVICE_AXES, None)
    return jax.shard_map(
        shards,
        mesh=grid,
        in_specs=(rows, rows, rows, rows, P(DEVICE_AXES)),
        out_specs=(rows, rows, rows, rows),
        check_vma=False,
    )
```

```python
import functools
import math

import jax
import jax.numpy as jnp
from jax import lax
from jax.experimental import pallas as pl
from jax.experimental.pallas import tpu as pltpu
from jax.sharding import Mesh, PartitionSpec as P

DH = 128
REACH = 4
PAIR = 2
CORE = 2
ROWS = 512
COLS = 512
STRIP = 32
PART = 256
MASKED = -1e6
CLEAR, MIXED = 0, 1
DEVICE_AXES = ("sup", "pair", "core", "head")
HEAD_AXES = ("head", "pair")
SEG_ROWS = 16
SECOND_FLOPS = 40_000_000_000
OUTPUTS = {"first": ("packed", "tag"), "second": ("sums", "sums", "tag"), "last": ("packed",)}
ATTEND_VMEM = 24 * 1024 * 1024
MOVE_VMEM = 8 * 1024 * 1024
PACK_VMEM = 63 * 1024 * 1024


def run_copies(copies):
    for copy in copies:
        copy.start()
    for copy in copies:
        copy.wait()


def listed(count):
    middle = range(count // 2, count // 2 + PAIR)
    return [*middle, *(index for index in range(count) if index not in middle)]


def pack_kernel(queries, keys, values, out_grad, segment, packed, *scratch):
    held, numbers, places, sems = scratch[:4], *scratch[4:]
    heads = packed.shape[0]
    tokens = queries.shape[0]

    def copies_in(order):
        return [
            pltpu.make_async_copy(source, held[slot], sems.at[0, slot])
            for slot, source in enumerate(order)
        ]

    def start(order):
        for copy in copies_in(order):
            copy.start()

    first_keys = lax.axis_index("sup") % 2 == 0
    by_keys, by_queries = (keys, values, queries, out_grad), (queries, out_grad, keys, values)
    numbers_in = pltpu.make_async_copy(segment, numbers, sems.at[0, 4])
    numbers_in.start()

    @pl.when(first_keys)
    def _():
        start(by_keys)

    @pl.when(jnp.logical_not(first_keys))
    def _():
        start(by_queries)

    def copy_out(part, at, rows):
        rows = pl.ds(at, rows)
        return pltpu.make_async_copy(places.at[:, rows], packed.at[:, rows], sems.at[1, part])

    numbers_in.wait()
    places[:, pl.ds(2 * tokens, SEG_ROWS)] = jnp.broadcast_to(
        (numbers[...] + 1).astype(jnp.float32).astype(places.dtype)[None], (heads, SEG_ROWS, tokens)
    )
    outs = []
    for slot, copy_in in enumerate(copies_in(by_keys)):
        copy_in.wait()
        at = slot * tokens + (SEG_ROWS if slot > 1 else 0)
        for head in range(heads):
            places[head, pl.ds(at, tokens)] = held[slot][:, pl.ds(head * DH, DH)]
        outs.append(copy_out(slot, at, tokens + (SEG_ROWS if slot == 1 else 0)))
        outs[-1].start()
    for copy in outs:
        copy.wait()


def pack(queries, keys, values, out_grad, segment):
    tokens, features = queries.shape
    shape = (features // DH, 4 * tokens + SEG_ROWS, DH)
    anywhere = pl.BlockSpec(memory_space=pl.ANY)
    return pl.pallas_call(
        pack_kernel,
        out_shape=jax.ShapeDtypeStruct(shape, queries.dtype),
        in_specs=[anywhere] * 5,
        out_specs=anywhere,
        scratch_shapes=[pltpu.VMEM(queries.shape, queries.dtype)] * 4
        + [
            pltpu.VMEM(segment.shape, segment.dtype),
            pltpu.VMEM(shape, queries.dtype),
            pltpu.SemaphoreType.DMA((2, 5)),
        ],
        compiler_params=pltpu.CompilerParams(vmem_limit_bytes=PACK_VMEM),
    )(queries, keys, values, out_grad, segment)


def unpack_kernel(queries_on, back, *refs):
    outs, rows_out, sems = refs[-6:-2], refs[-2], refs[-1]
    heads = back.shape[0]
    tokens = rows_out.shape[1]
    of_queries = lax.axis_index("sup") % 2 == queries_on

    def copy_out(slot, target):
        return pltpu.make_async_copy(rows_out.at[slot], target, sems.at[slot])

    for slot, (by_query, by_key) in enumerate(((outs[0], outs[3]), (outs[1], outs[2]))):
        for head in range(heads):
            rows_out[slot, :, pl.ds(head * DH, DH)] = back[head, pl.ds(slot * tokens, tokens)]
        pl.when(of_queries)(lambda: copy_out(slot, by_query).start())
        pl.when(jnp.logical_not(of_queries))(lambda: copy_out(slot, by_key).start())
    for slot in range(2):
        copy_out(slot, outs[slot]).wait()


def unpack(queries_on, back, outs=()):
    heads, rows, _ = back.shape
    tokens = rows // 2
    anywhere = pl.BlockSpec(memory_space=pl.ANY)
    return pl.pallas_call(
        functools.partial(unpack_kernel, queries_on),
        out_shape=[jax.ShapeDtypeStruct((tokens, heads * DH), back.dtype)] * 4,
        in_specs=[pl.BlockSpec(memory_space=pltpu.VMEM)] + [anywhere] * len(outs),
        out_specs=[anywhere] * 4,
        scratch_shapes=[
            pltpu.VMEM((2, tokens, heads * DH), back.dtype),
            pltpu.SemaphoreType.DMA((2,)),
        ],
        input_output_aliases={1 + i: i for i in range(len(outs))},
        compiler_params=pltpu.CompilerParams(vmem_limit_bytes=MOVE_VMEM),
    )(back, *outs)


def attend_kernel(factors, slabs, step_name, own_seg, other_seg, rows_slab, *refs):
    score_scale, norm = factors
    forward, skipped = step_name == "first", 2 if step_name == "last" else 0
    col_slabs, refs = refs[: 2 * slabs - skipped], refs[2 * slabs - skipped :]
    given, outs = refs[: -11 - len(OUTPUTS[step_name])], refs[-11 - len(OUTPUTS[step_name]) : -11]
    seg, seg_rows, seg_cols, row_one, row_two, col_one, col_two = refs[-11:-4]
    sum_one, sum_two, work, sem = refs[-4:]
    parity, core = lax.axis_index("sup") % 2, lax.axis_index("core")
    sign = (1 - 2 * parity) * (1 if forward else -1)
    chunks = rows_slab.shape[0]
    tokens = own_seg.shape[2]
    half_rows = chunks // PAIR * tokens
    half_blocks = half_rows // COLS
    local_blocks = REACH * half_blocks
    row_blocks = chunks * tokens // ROWS
    col_chunks = COLS // tokens
    first_block = local_blocks if skipped else 0
    if step_name == "first":
        outs[1][...] = jnp.zeros_like(outs[1])
    if step_name == "second":
        outs[2][...] = given[0][...]

    def place_of(index, chunk):
        slab, owner = index // 2, (core if index % 2 == 0 else 1 - core)
        inner, pair = divmod(listed(chunks)[chunk], PAIR)
        return (slab * REACH + pair * CORE + owner) * (chunks // PAIR) + inner

    def row_of(chunk):
        inner, pair = divmod(listed(chunks)[chunk], PAIR)
        return (pair * (chunks // PAIR) + inner) * tokens

    for index in range(2 * slabs):
        local = index < 2
        source = (own_seg, other_seg)[index] if local else col_slabs[index - skipped]
        at = 0 if local else 2 * tokens
        for chunk in range(chunks):
            numbers = source[chunk, pl.ds(at, SEG_ROWS)].astype(jnp.float32)[:1]
            place = place_of(index, chunk)
            lanes = pl.ds(row_of(chunk) % COLS, tokens)
            seg_cols[place // col_chunks, :, lanes] = numbers.astype(jnp.int32)
    to_scalars = pltpu.make_async_copy(seg_cols, seg, sem)
    to_scalars.start()
    for index, source in enumerate(col_slabs, skipped):
        for chunk in range(chunks):
            place = place_of(index, chunk) - first_block * col_chunks
            rows = pl.ds(row_of(chunk) % COLS, tokens)
            for slot, ref in enumerate((col_one, col_two)):
                ref[place // col_chunks, rows] = source[chunk, pl.ds(slot * tokens, tokens)]
    for chunk in range(chunks):
        for slot, ref in enumerate((row_one, row_two)):
            ref[pl.ds(row_of(chunk), tokens)] = rows_slab[chunk, pl.ds(slot * tokens, tokens)]

    def row_token_of(row_block):
        row_start = row_block * ROWS
        return (row_start // half_rows * CORE + core) * half_rows + row_start % half_rows

    def col_token_of(block):
        beyond = jnp.where(block >= local_blocks, 1, 0)
        return block * COLS - beyond * (sign + 1) * local_blocks * COLS

    def seg_at(token):
        return seg[token // COLS, 0, token % COLS]

    for index, ref in enumerate((sum_one, sum_two)):
        ref[...] = given[index][...] if step_name == "last" else jnp.zeros_like(ref)
    to_scalars.wait()
    total = 0
    for row_block in range(row_blocks):
        row_token = row_token_of(row_block)
        row_first, row_last = seg_at(row_token), seg_at(row_token + ROWS - 1)
        at_rows = row_block * ROWS

        @pl.when(row_first == row_last)
        def _():
            seg_rows[pl.ds(at_rows, ROWS)] = jnp.full((ROWS, DH), row_first, jnp.int32)

        @pl.when(row_first != row_last)
        def _():
            for chunk in range(chunks):
                if row_of(chunk) // ROWS != row_block:
                    continue
                numbers = own_seg[chunk].astype(jnp.float32)[:1]
                seg_rows[pl.ds(row_of(chunk), tokens)] = jnp.transpose(
                    jnp.broadcast_to(numbers, (DH, tokens))
                ).astype(jnp.int32)

        for block in range(first_block, slabs * local_blocks):
            col_token = col_token_of(block)
            col_first, col_last = seg[block, 0, 0], seg[block, 0, COLS - 1]
            touching = (col_last >= row_first) & (col_first <= row_last)
            ahead, behind = col_token - row_token, row_token + ROWS - col_token
            reached = jnp.where(sign > 0, behind > 0, ahead + COLS > 0)
            inside = jnp.where(sign > 0, ahead + COLS <= 1, behind <= 1)
            same = (row_first == row_last) & (col_first == row_first) & (col_last == row_first)
            work[0, total] = row_block
            work[1, total] = block
            work[2, total] = jnp.where(same & inside, CLEAR, MIXED)
            total = total + jnp.where(touching & reached, 1, 0)
    dims = (((1,), (1,)), ((), ()))

    def weigh(raw, dprob):
        logistic = pltpu.reciprocal(
            1.0 + jnp.exp2(raw * (-score_scale * math.log2(math.e))), approx=True
        )
        active = raw * logistic
        slope = logistic + active * score_scale * (1.0 - logistic)
        return (active * (score_scale * norm)).astype(jnp.bfloat16), (dprob * slope).astype(
            jnp.bfloat16
        )

    def tile(item, masked):
        row_block, block = work[0, item], work[1, item]
        held = block - first_block
        if masked:
            offset = (col_token_of(block) - row_token_of(row_block)) * sign
            distance = (
                lax.broadcasted_iota(jnp.int32, (STRIP, DH), 0)
                - lax.broadcasted_iota(jnp.int32, (STRIP, DH), 1)
            ) * sign
        for part in range(0, ROWS, PART):
            at = pl.ds(pl.multiple_of(row_block * ROWS + part, PART), PART)
            scores, dprobs = [
                lax.dot_general(rows[at], cols[held], dims, preferred_element_type=jnp.float32)
                for rows, cols in ((row_one, col_one), (row_two, col_two))
            ]
            weights, dscores = [], []
            for row in range(0, PART, STRIP):
                pieces = []
                if masked:
                    row_seg = seg_rows[pl.ds(row_block * ROWS + part + row, STRIP)]
                for col in range(0, COLS, DH):
                    raw = scores[row : row + STRIP, col : col + DH]
                    if masked:
                        col_seg = jnp.broadcast_to(seg_cols[block, :, pl.ds(col, DH)], (STRIP, DH))
                        allowed = (row_seg == col_seg) & (
                            distance >= offset - (part + row - col) * sign
                        )
                        raw = jnp.where(allowed, raw, MASKED)
                    pieces.append(weigh(raw, dprobs[row : row + STRIP, col : col + DH]))
                weights.append(jnp.concatenate([piece[0] for piece in pieces], axis=1))
                dscores.append(jnp.concatenate([piece[1] for piece in pieces], axis=1))
            for target, left, cols in ((sum_one, weights, col_two), (sum_two, dscores, col_one)):
                target[row_block, pl.ds(part, PART)] += jnp.dot(
                    jnp.concatenate(left, axis=0), cols[held], preferred_element_type=jnp.float32
                )

    def step(item, carry):
        clear = work[2, item] == CLEAR
        pl.when(clear)(functools.partial(tile, item, False))
        pl.when(jnp.logical_not(clear))(functools.partial(tile, item, True))
        return carry

    lax.fori_loop(0, total, step, 0)
    if step_name == "second":
        outs[0][...] = sum_one[...]
        outs[1][...] = sum_two[...]
        return
    packed = outs[0]
    for chunk in range(chunks):
        row_block, inner = row_of(chunk) // ROWS, row_of(chunk) % ROWS
        at = pl.ds(inner, tokens)
        packed[chunk, pl.ds(0, tokens)] = sum_one[row_block, at].astype(packed.dtype)
        packed[chunk, pl.ds(tokens, tokens)] = (
            sum_two[row_block, at] * (norm * score_scale)
        ).astype(packed.dtype)


def attend(step_name, rows_slab, col_slabs, local_segs, given=()):
    chunks = rows_slab.shape[0]
    rows = chunks * DH
    skipped = 2 if step_name == "last" else 0
    slabs = (len(col_slabs) + skipped) // 2
    reach = CORE * rows
    factors = (1.0 / math.sqrt(DH), 1.0 / math.sqrt(reach))
    vmem = pl.BlockSpec(memory_space=pltpu.VMEM)
    dtype = rows_slab.dtype
    blocks = slabs * reach // COLS
    row_blocks = rows // ROWS
    outputs = {
        "packed": jax.ShapeDtypeStruct((chunks, 2 * rows // chunks, DH), dtype),
        "sums": jax.ShapeDtypeStruct((row_blocks, ROWS, DH), jnp.float32),
        "tag": jax.ShapeDtypeStruct((1, 1, DH), jnp.float32),
    }
    outputs = [outputs[name] for name in OUTPUTS[step_name]]
    flops = {"first": 8 * DH * rows * reach * slabs, "second": SECOND_FLOPS, "last": 0}[step_name]
    return pl.pallas_call(
        functools.partial(attend_kernel, factors, slabs, step_name),
        out_shape=outputs,
        in_specs=[vmem] * (3 + len(col_slabs) + len(given)),
        out_specs=[vmem] * len(outputs),
        scratch_shapes=[
            pltpu.SMEM((blocks, 1, COLS), jnp.int32),
            pltpu.VMEM((rows, DH), jnp.int32),
            pltpu.VMEM((blocks, 1, COLS), jnp.int32),
            pltpu.VMEM((rows, DH), dtype),
            pltpu.VMEM((rows, DH), dtype),
            pltpu.VMEM((len(col_slabs) * rows // COLS, COLS, DH), dtype),
            pltpu.VMEM((len(col_slabs) * rows // COLS, COLS, DH), dtype),
        ]
        + [
            pltpu.VMEM((row_blocks, ROWS, DH), jnp.float32),
            pltpu.VMEM((row_blocks, ROWS, DH), jnp.float32),
            pltpu.SMEM((3, row_blocks * blocks + 1), jnp.int32),
            pltpu.SemaphoreType.DMA(()),
        ],
        compiler_params=pltpu.CompilerParams(vmem_limit_bytes=ATTEND_VMEM),
        cost_estimate=pl.CostEstimate(flops=flops, bytes_accessed=0, transcendentals=0),
    )(*local_segs, rows_slab, *col_slabs, *given)


def shards(queries, keys, values, out_grad, segment):
    sups = lax.axis_size("sup")
    tokens = queries.shape[0]

    def over_heads(packed):
        return lax.all_to_all(
            packed,
            HEAD_AXES,
            split_axis=0,
            concat_axis=0,
            axis_index_groups=[listed(packed.shape[0])],
            tiled=True,
        )

    def with_other_core(slab):
        return [slab, lax.ppermute(slab, "core", [(0, 1), (1, 0)])]

    def over_sups(slab, start):
        pairs = [(i, i + 1) for i in range(start, sups - 1, 2)]
        return lax.ppermute(slab, "sup", pairs + [(b, a) for a, b in pairs])

    slab = over_heads(pack(queries, keys, values, out_grad, segment[None]))
    first_own, second_own = slab[:, : 2 * tokens + SEG_ROWS], slab[:, 2 * tokens + SEG_ROWS :]
    first_cols = with_other_core(first_own)
    beyond = over_sups(first_own, 0)
    second_cols = with_other_core(second_own)
    local_segs = [slab[:, 2 * tokens :] for slab in first_cols]
    first_all = first_cols
    if sups > 2:
        later = over_sups(jnp.concatenate([second_own, local_segs[0]], axis=1), 1)
        first_all = first_cols + with_other_core(later)
    first_sums, tag = attend("first", second_own, first_all, local_segs)
    first_back = over_heads(first_sums)
    *local_sums, tag = attend("second", first_own, second_cols, local_segs, (tag,))
    beyond_cols = with_other_core(beyond + tag.astype(beyond.dtype))
    (second_sums,) = attend("last", first_own, beyond_cols, local_segs, local_sums)
    second_back = over_heads(second_sums)
    return tuple(unpack(1, second_back, unpack(0, first_back)))


def solution(mesh):
    blocks = mesh.shape["grp"] * mesh.shape["blk"]
    grid = Mesh(
        mesh.devices.reshape(blocks // REACH, PAIR, CORE, mesh.shape["head"]), DEVICE_AXES
    )
    rows = P(DEVICE_AXES, None)
    return jax.shard_map(
        shards,
        mesh=grid,
        in_specs=(rows, rows, rows, rows, P(DEVICE_AXES)),
        out_specs=(rows, rows, rows, rows),
        check_vma=False,
    )
```
